256 devices in a mesh: wide: 32 (over x, y, z_hi), narrow: 8 (over z_lo, core).
Axes of the slice: x: 4, y: 4, z: 8 (z_hi: 2, z_lo: 4; z = z_hi * 4 + z_lo), core: 2. Of those that a mesh axis runs over, the one named last changes fastest.
Arguments:
- tokens: bfloat16 [2, 256, 9216], P(None, None, 'narrow'), may hold values from -6 to 6
- gate_weight: bfloat16 [36864, 9216], P(('wide', 'narrow')), may hold values from -0.0625 to 0.0625
- up_weight: bfloat16 [36864, 9216], P(('wide', 'narrow')), may hold values from -0.0625 to 0.0625
- down_weight: bfloat16 [36864, 9216], P('wide', 'narrow'), may hold values from -0.03125 to 0.03125
Outputs:
- mixed: bfloat16 [2, 256, 9216], P(None, 'wide', 'narrow')
The draws below stay inside these ranges and needn't reach their ends.
All inputs are finite; a program needn't handle non-finite values.
Results may differ from the reference program's by a relative error of at most 0.0049.
Values may be sent and summed in bfloat16 or wider, within the bound.
No kernel may reach another device: no remote copies, remote signals or barrier semaphores. Data moves between devices by JAX's collectives and lax.ppermute only.
A program may use at most 64 MiB of HBM per device.

```python
import jax
import jax.numpy as jnp
from jax import lax

D = 9216
FF = 36864
ROWS_MB = 256


def levels(rng, extent, split, low, largest):
    def one(axis_at, shards_of):
        draws = jax.random.uniform(jax.random.fold_in(jax.random.fold_in(rng, 6), axis_at), (shards_of,), jnp.float32, low / len(split), largest / len(split))
        return jnp.repeat(jnp.exp(draws), extent[axis_at] // shards_of).reshape((-1,) + (1,) * (len(extent) - axis_at - 1))

    factor_of = one(*split[0])
    for cut in split[1:]:
        factor_of = factor_of * one(*cut)
    return factor_of


def gaussian(rng, extent, width, limit, shards=(), kind=jnp.bfloat16):
    result = width * jax.random.normal(rng, extent, jnp.float32)
    if shards:
        result = result * levels(rng, extent, shards, -0.22, 0.18)
    return jnp.clip(result, -limit, limit).astype(kind)


def setup_inputs(seed: int = 0) -> dict:
    streams_of = jax.random.split(jax.random.key(seed), 5)
    tokens = gaussian(streams_of[0], (2, ROWS_MB, D), 1.0, 6.0, ((2, 8),))
    gate_weight = gaussian(streams_of[1], (FF, D), D ** -0.5, 0.0625, ((0, 256),))
    up_weight = gaussian(streams_of[2], (FF, D), D ** -0.5, 0.0625, ((0, 256),))
    down_weight = gaussian(streams_of[3], (FF, D), FF ** -0.5, 0.03125, ((0, 32), (1, 8)))
    return dict(tokens=tokens, gate_weight=gate_weight, up_weight=up_weight, down_weight=down_weight)


def reference(tokens, gate_weight, up_weight, down_weight):
    def layer(rows):
        gate = jnp.dot(rows, gate_weight.T, preferred_element_type=jnp.float32)
        up = jnp.dot(rows, up_weight.T, preferred_element_type=jnp.float32)
        hidden = (jax.nn.silu(gate) * up).astype(jnp.bfloat16)
        return jnp.dot(hidden, down_weight, preferred_element_type=jnp.float32).astype(jnp.bfloat16)

    return lax.map(layer, tokens)
```

```python
import jax
import jax.numpy as jnp
import numpy as np
from jax import lax
from jax.sharding import Mesh, PartitionSpec as P

AXES = ("x", "y", "h", "l", "c")
SIZES = (4, 4, 2, 4, 2)
F32 = jnp.float32
BF16 = jnp.bfloat16


def _perm(move):
    pairs = []
    for source in range(256):
        x, y, h, l, c = (int(i) for i in np.unravel_index(source, SIZES))
        X, Y, Z, C = move(x, y, h * 4 + l, c)
        Z %= 8
        pairs.append((source, int(np.ravel_multi_index((X % 4, Y % 4, Z // 4, Z % 4, C % 2), SIZES))))
    return pairs


def _permute(a, move):
    return lax.ppermute(a, AXES, _perm(move))


def _first(k):
    return lambda x, y, z, c: (x + k, y, z, c) if c == 0 else (x, y + k, z, c)


def _second(k):
    return lambda x, y, z, c: (x, y + k, z, c) if c == 0 else (x + k, y, z, c)


def _swap(x, y, z, c):
    return (x, y, z, 1 - c)


def _z(k):
    return lambda x, y, z, c: (x, y, z + k, c)


def _z_two(x, y, z, c):
    return (x, y, z + 2 if c == 0 else z - 2, c)


def _lo(k):
    return lambda x, y, z, c: (x, y, (z // 4) * 4 + (z % 4 + k) % 4, c)


def local(tokens, gate_weight, up_weight, down_weight):
    x, y, h, l, c = (lax.axis_index(a) for a in AXES)
    core0 = c == 0
    width = tokens.shape[-1]
    units = gate_weight.shape[0]

    gate_other = _permute(gate_weight, _swap)
    up_other = _permute(up_weight, _swap)

    t0 = tokens[0]
    t1 = tokens[1].reshape(4, 4, 16, width).transpose(1, 0, 2, 3).reshape(256, width)
    mine = jnp.where(core0, t0, t1)
    theirs = jnp.where(core0, t1, t0)
    other = _permute(theirs, _swap)
    own = jnp.concatenate([jnp.where(core0, mine, other), jnp.where(core0, other, mine)], axis=1)

    q = jnp.where(core0, x + 2 * y, 2 * x + y) % 4
    own2 = jnp.concatenate([own, own], axis=0)
    own = lax.dynamic_slice_in_dim(own2, q * 64, 256, axis=0)
    quarter = own[:64]

    from_up = _permute(quarter, _z(-1))
    from_down = _permute(quarter, _z(1))
    from_two = _permute(quarter, _z_two)
    down_other = _permute(down_weight, _swap)

    bundle = jnp.concatenate([from_up, from_two, from_down], axis=1)
    next1 = _permute(bundle, _first(-1))
    next3 = _permute(bundle, _first(1))
    next2a = _permute(bundle[:32], _second(-1))
    next2b = _permute(bundle[32:], _second(1))
    rest = jnp.concatenate([bundle, next1, next2a, next2b, next3], axis=0)

    w = jnp.concatenate(
        [
            jnp.where(core0, gate_weight, gate_other),
            jnp.where(core0, gate_other, gate_weight),
            jnp.where(core0, up_weight, up_other),
            jnp.where(core0, up_other, up_weight),
        ],
        axis=0,
    )
    block = 2 * width
    w2 = jnp.concatenate([w, w], axis=1)
    w = lax.dynamic_slice_in_dim(w2, l * block, 4 * block, axis=1)

    both = jnp.einsum("bk,fk->bf", own, w[:, :block], preferred_element_type=F32)
    both = both + jnp.einsum("bk,fk->bf", rest, w[:, block:], preferred_element_type=F32)
    gate, up = both[:, : 2 * units], both[:, 2 * units :]
    hidden = (jax.nn.silu(gate) * up).astype(BF16)

    hs = [hidden] + [_permute(hidden, _lo(-k)) for k in (1, 2, 3)]
    dw = jnp.concatenate([down_weight, down_other], axis=1)
    dw = lax.dynamic_slice_in_dim(jnp.concatenate([dw, dw], axis=0), l * 2 * units, 8 * units, axis=0)
    part = jnp.einsum("bf,fd->bd", jnp.concatenate(hs, axis=1), dw, preferred_element_type=F32)

    p = jnp.where(core0, y, x) % 2
    part = part.reshape(4, 64, 2 * width)

    def to(k):
        return lax.dynamic_index_in_dim(part, (k + 2 * p) % 4, 0, keepdims=False)

    stage = to(0)
    got = [_permute(to(k).astype(BF16), _first(k)) for k in (1, 3, 2)]
    for g in got:
        stage = stage + g.astype(F32)
    stage = stage.reshape(4, 16, 2 * width)
    s2 = jnp.where(core0, y, x)

    def to2(k):
        return lax.dynamic_index_in_dim(stage, (s2 + k) % 4, 0, keepdims=False)

    last = to2(0)
    got = [_permute(to2(k).astype(BF16), _second(k)) for k in (1, 3, 2)]
    for g in got:
        last = last + g.astype(F32)
    last = last.reshape(2, 8, 2 * width)
    here = lax.dynamic_index_in_dim(last, h, 0, keepdims=False)
    there = lax.dynamic_index_in_dim(last, 1 - h, 0, keepdims=False)
    a = _permute(there[:, :width], _z(4))
    b = _permute(here[:, width:], _swap)
    d = _permute(there[:, width:], lambda x, y, z, c: (x, y, z + 4, 1 - c))
    same = (here[:, :width] + a).astype(BF16)
    cross = (b + d).astype(BF16)
    return jnp.stack([jnp.where(core0, same, cross), jnp.where(core0, cross, same)])


def solution(mesh):
    fine = Mesh(mesh.devices.reshape(SIZES), AXES)
    wide, narrow = ("x", "y", "h"), ("l", "c")
    return jax.shard_map(
        local,
        mesh=fine,
        in_specs=(
            P(None, None, narrow),
            P(wide + narrow, None),
            P(wide + narrow, None),
            P(wide, narrow),
        ),
        out_specs=P(None, wide, narrow),
        check_vma=False,
    )
```

```python
import functools

import jax
import jax.numpy as jnp
import numpy as np
from jax import lax
from jax.experimental import pallas as pl
from jax.experimental.pallas import tpu as pltpu
from jax.sharding import Mesh, PartitionSpec as P

AXES = ("x", "y", "h", "l", "c")
SIZES = (4, 4, 2, 4, 2)
F32 = jnp.float32
BF16 = jnp.bfloat16
MIB = 1 << 20


def _perm(move):
    pairs = []
    for source in range(256):
        x, y, h, l, c = (int(i) for i in np.unravel_index(source, SIZES))
        X, Y, Z, C = move(x, y, h * 4 + l, c)
        Z %= 8
        pairs.append((source, int(np.ravel_multi_index((X % 4, Y % 4, Z // 4, Z % 4, C % 2), SIZES))))
    return pairs


def _permute(a, move):
    return lax.ppermute(a, AXES, _perm(move))


def _first(k):
    return lambda x, y, z, c: (x + k, y, z, c) if c == 0 else (x, y + k, z, c)


def _second(k):
    return lambda x, y, z, c: (x, y + k, z, c) if c == 0 else (x + k, y, z, c)


def _swap(x, y, z, c):
    return (x, y, z, 1 - c)


def _z(k):
    return lambda x, y, z, c: (x, y, z + k, c)


def _z_two(x, y, z, c):
    return (x, y, z + 2 if c == 0 else z - 2, c)


def _lo(k):
    return lambda x, y, z, c: (x, y, (z // 4) * 4 + (z % 4 + k) % 4, c)


VMEM = functools.partial(pl.BlockSpec, memory_space=pltpu.VMEM)
ANY = pl.BlockSpec(memory_space=pl.ANY)
SMEM = pl.BlockSpec(memory_space=pltpu.SMEM)


def _order_kernel(place, tokens, mine, theirs):
    for half, out in ((0, mine), (1, theirs)):
        batch = place[half]
        q = place[2 + half]
        for i in range(4):
            a = lax.rem(q + i, 4)
            for j in range(4):
                block = jnp.where(batch == 0, a * 4 + j, j * 4 + a)
                row = pl.multiple_of(block * 16, 16)
                out[pl.ds((i * 4 + j) * 16, 16), :] = tokens[batch, pl.ds(row, 16), :]


def _order(place, tokens):
    _, rows, width = tokens.shape
    shape = jax.ShapeDtypeStruct((rows, width), BF16)
    return pl.pallas_call(
        _order_kernel,
        in_specs=[SMEM, VMEM()],
        out_specs=[VMEM(), VMEM()],
        out_shape=[shape, shape],
        name="order_rows",
    )(place, tokens)


def _load_weights(offsets, weights, buffer, sems, blocks):
    units = weights[0].shape[0]
    width = buffer.shape[-1]
    copies = []
    for k in range(blocks):
        column = pl.multiple_of(offsets[k] * width, 128)
        copies.append(
            [
                pltpu.make_async_copy(
                    w.at[:, pl.ds(column, width)],
                    buffer.at[k, pl.ds(i * units, units), :],
                    sems.at[k, i],
                )
                for i, w in enumerate(weights)
            ]
        )
    for step in copies:
        for copy in step:
            copy.start()
    return copies


def _dot_t(w, t):
    return lax.dot_general(w, t, (((1,), (1,)), ((), ())), preferred_element_type=F32)


def _own_kernel(offsets, mine, other, g0, g1, u0, u1, out, buffer, sems):
    copies = _load_weights(offsets, (g0, g1, u0, u1), buffer, sems, 2)
    for k, t in enumerate((mine, other)):
        for copy in copies[k]:
            copy.wait()
        part = _dot_t(buffer[k], t[...])
        if k == 0:
            out[...] = part
        else:
            out[...] += part


def _own(offsets, mine, other, weights):
    units, (rows, width) = weights[0].shape[0], mine.shape
    return pl.pallas_call(
        _own_kernel,
        in_specs=[SMEM, VMEM(), VMEM()] + [ANY] * 4,
        out_specs=VMEM(),
        out_shape=jax.ShapeDtypeStruct((4 * units, rows), F32),
        scratch_shapes=[pltpu.VMEM((2, 4 * units, width), BF16), pltpu.SemaphoreType.DMA((2, 4))],
        compiler_params=pltpu.CompilerParams(vmem_limit_bytes=16 * MIB),
        cost_estimate=pl.CostEstimate(
            flops=2 * 8 * units * rows * width, bytes_accessed=20 * units * width, transcendentals=0
        ),
        name="own_features",
    )(offsets, mine, other, *weights)


def _hidden_kernel(offsets, tokens, start, g0, g1, u0, u1, out, acc, buffer, sems):
    copies = _load_weights(offsets, (g0, g1, u0, u1), buffer, sems, 6)
    units = g0.shape[0]
    for k in range(6):
        for copy in copies[k]:
            copy.wait()
        part = _dot_t(buffer[k], tokens[k])
        if k == 0:
            acc[...] = start[...] + part
        else:
            acc[...] += part
    gate = acc[pl.ds(0, 2 * units), :]
    up = acc[pl.ds(2 * units, 2 * units), :]
    hidden = (gate / (1 + jnp.exp(-gate)) * up).astype(BF16)
    half = hidden.shape[1] // 2
    odd = offsets[6] == 1
    a, b = hidden[:, :half], hidden[:, half:]
    out[:, :half] = jnp.where(odd, b, a)
    out[:, half:] = jnp.where(odd, a, b)


def _hidden(offsets, tokens, start, weights):
    units, (blocks, rows, width) = weights[0].shape[0], tokens.shape
    return pl.pallas_call(
        _hidden_kernel,
        in_specs=[SMEM, VMEM(), VMEM()] + [ANY] * 4,
        out_specs=VMEM(),
        out_shape=jax.ShapeDtypeStruct((2 * units, rows), BF16),
        scratch_shapes=[
            pltpu.VMEM((4 * units, rows), F32),
            pltpu.VMEM((blocks, 4 * units, width), BF16),
            pltpu.SemaphoreType.DMA((blocks, 4)),
        ],
        compiler_params=pltpu.CompilerParams(vmem_limit_bytes=24 * MIB),
        cost_estimate=pl.CostEstimate(
            flops=2 * 4 * blocks * units * rows * width,
            bytes_accessed=8 * blocks * units * width,
            transcendentals=2 * units * rows,
        ),
        name="gate_up_silu",
    )(offsets, tokens, start, *weights)


COLUMNS = 384


def _down_kernel(place, h0, h1, h2, h3, d0, d1, own, s1, s2, s3, ht, buffer, sems):
    width = d0.shape[1]
    tiles = width // COLUMNS
    units = h0.shape[0] // 2
    copies = []
    for i, d in enumerate((d0, d1)):
        for n in range(tiles):
            copies.append(
                pltpu.make_async_copy(
                    d.at[:, pl.ds(n * COLUMNS, COLUMNS)], buffer.at[i * tiles + n], sems.at[i * tiles + n]
                )
            )
    for copy in copies:
        copy.start()
    l, c = place[0], place[1]
    for k, part in enumerate((h0, h1, h2, h3)):
        base = lax.rem(l + k, 4) * (2 * units)
        for i, core in enumerate((c, 1 - c)):
            row = pl.multiple_of(base + core * units, 16)
            ht[pl.ds(row, units), :] = part[pl.ds(i * units, units), :]
    hidden = ht[...].T
    block = hidden.shape[0] // 4
    for i in range(2):
        for n in range(tiles):
            copies[i * tiles + n].wait()
            result = jnp.dot(hidden, buffer[i * tiles + n], preferred_element_type=F32)
            columns = pl.ds(n * COLUMNS, COLUMNS)
            own[i, :, columns] = result[:block]
            for k, out in enumerate((s1, s2, s3)):
                out[i, :, columns] = result[(k + 1) * block : (k + 2) * block].astype(BF16)


def _down(place, hs, d0, d1):
    units2, rows = hs[0].shape
    depth, width = d0.shape
    block = rows // 4
    tiles = 2 * width // COLUMNS
    send = jax.ShapeDtypeStruct((2, block, width), BF16)
    return pl.pallas_call(
        _down_kernel,
        in_specs=[SMEM] + [VMEM()] * 4 + [ANY] * 2,
        out_specs=[VMEM()] * 4,
        out_shape=[jax.ShapeDtypeStruct((2, block, width), F32), send, send, send],
        scratch_shapes=[
            pltpu.VMEM((depth, rows), BF16),
            pltpu.VMEM((tiles, depth, COLUMNS), BF16),
            pltpu.SemaphoreType.DMA((tiles,)),
        ],
        compiler_params=pltpu.CompilerParams(vmem_limit_bytes=24 * MIB),
        cost_estimate=pl.CostEstimate(
            flops=4 * rows * depth * width, bytes_accessed=4 * depth * width, transcendentals=0
        ),
        name="down",
    )(place, *hs, d0, d1)


def local(tokens, gate_weight, up_weight, down_weight):
    x, y, h, l, c = (lax.axis_index(a).astype(jnp.int32) for a in AXES)
    core0 = c == 0
    width = tokens.shape[-1]

    q0, q1 = (x + 2 * y) % 4, (2 * x + y) % 4
    place = jnp.stack([c, 1 - c, jnp.where(core0, q0, q1), jnp.where(core0, q1, q0)])
    s2 = jnp.where(core0, y, x)
    ahead = [((l + k) % 4) * 2 for k in range(4)]
    columns_own = jnp.stack([ahead[0] + c, ahead[0] + 1 - c])
    columns = jnp.stack([o for a in ahead[1:] for o in (a + c, a + 1 - c)] + [s2 % 2])

    mine, theirs = _order(place, tokens)
    other = _permute(theirs, _swap)
    gate_other = _permute(gate_weight, _swap)
    up_other = _permute(up_weight, _swap)

    quarter = jnp.stack([mine[:64], other[:64]])
    from_up = _permute(quarter, _z(-1))
    from_down = _permute(quarter, _z(1))
    from_two = _permute(quarter, _z_two)
    down_in, _ = lax.optimization_barrier((down_weight, from_up))
    down_other = _permute(down_in, _swap)

    bundle = jnp.concatenate([from_up, from_two, from_down], axis=0)
    bundle, gate_other, up_other = lax.optimization_barrier((bundle, gate_other, up_other))
    weights = (gate_weight, gate_other, up_weight, up_other)
    next1 = _permute(bundle, _first(-1))
    next3 = _permute(bundle, _first(1))
    next2a = _permute(bundle[:, :32], _second(-1))
    next2b = _permute(bundle[:, 32:], _second(1))
    start = _own(columns_own, mine, other, weights)
    rest = jnp.concatenate([bundle, next1, next2a, next2b, next3], axis=1)

    hidden = _hidden(columns, rest, start, weights)
    hs = [hidden] + [_permute(hidden, _lo(-k)) for k in (1, 2, 3)]

    own, *sends = _down(jnp.stack([l, c]), hs, down_weight, down_other)
    got = [_permute(s, _first(k)) for s, k in zip(sends, (1, 2, 3))]
    stage = own
    for g in got:
        stage = stage + g.astype(F32)
    stage = stage.reshape(2, 4, 16, width)

    def to2(k):
        return lax.dynamic_index_in_dim(stage, (s2 + k) % 4, 1, keepdims=False)

    last = to2(0)
    got = [_permute(to2(k).astype(BF16), _second(k)) for k in (1, 2, 3)]
    for g in got:
        last = last + g.astype(F32)

    cross = _permute(last[1], _swap)
    both = jnp.stack([jnp.where(core0, last[0], cross), jnp.where(core0, cross, last[0])])
    both = both.reshape(2, 2, 8, width)
    here = lax.dynamic_index_in_dim(both, h, 1, keepdims=False)
    there = lax.dynamic_index_in_dim(both, 1 - h, 1, keepdims=False)
    return (here + _permute(there, _z(4))).astype(BF16)


def solution(mesh):
    fine = Mesh(mesh.devices.reshape(SIZES), AXES)
    wide, narrow = ("x", "y", "h"), ("l", "c")
    return jax.shard_map(
        local,
        mesh=fine,
        in_specs=(
            P(None, None, narrow),
            P(wide + narrow, None),
            P(wide + narrow, None),
            P(wide, narrow),
        ),
        out_specs=P(None, wide, narrow),
        check_vma=False,
    )
```

```python
import jax
import jax.numpy as jnp
import numpy as np
from jax import lax
from jax.experimental import pallas as pl
from jax.experimental.pallas import tpu as pltpu
from jax.sharding import Mesh, PartitionSpec as P

AXES = ("x", "y", "h", "l", "c")
SIZES = (4, 4, 2, 4, 2)
F32 = jnp.float32
BF16 = jnp.bfloat16
MIB = 1 << 20


def _perm(move):
    pairs = []
    for source in range(256):
        x, y, h, l, c = (int(i) for i in np.unravel_index(source, SIZES))
        X, Y, Z, C = move(x, y, h * 4 + l, c)
        Z %= 8
        pairs.append((source, int(np.ravel_multi_index((X % 4, Y % 4, Z // 4, Z % 4, C % 2), SIZES))))
    return pairs


def _permute(a, move):
    return lax.ppermute(a, AXES, _perm(move))


def _first(k):
    return lambda x, y, z, c: (x + k, y, z, c) if c == 0 else (x, y + k, z, c)


def _second(k):
    return lambda x, y, z, c: (x, y + k, z, c) if c == 0 else (x + k, y, z, c)


def _swap(x, y, z, c):
    return (x, y, z, 1 - c)


def _z(k):
    return lambda x, y, z, c: (x, y, z + k, c)


def _z_two(x, y, z, c):
    return (x, y, z + 2 if z % 2 == 0 else z - 2, c)


def _lo(k):
    return lambda x, y, z, c: (x, y, (z // 4) * 4 + (z % 4 + k) % 4, c)


def _only(core, move):
    return [(s, d) for s, d in _perm(move) if s % 2 == core]


VMEM = pl.BlockSpec(memory_space=pltpu.VMEM)
NT = (((1,), (1,)), ((), ()))


def _place():
    return [lax.axis_index(a).astype(jnp.int32) for a in AXES]


def _along(core, x, y):
    return jnp.where(core == 0, x, y), jnp.where(core == 0, y, x)


def _order_kernel(tokens, mine, theirs):
    x, y, _, _, c = _place()
    for core, out in ((c, mine), (1 - c, theirs)):
        first, second = _along(core, x, y)
        for half, q in enumerate((first + 2 * second, 2 * first + second)):
            for i in range(4):
                a = lax.rem(q + i, 4)
                base = 64 + half * 96 + (i - 1) * 32 if i else half * 32
                for j in range(2):
                    b = 2 * half + j
                    block = jnp.where(core == 0, a * 4 + b, b * 4 + a)
                    row = pl.multiple_of(block * 16, 16)
                    out[pl.ds(base + j * 16, 16), :] = tokens[core, pl.ds(row, 16), :]


def _order(tokens):
    _, rows, width = tokens.shape
    shape = jax.ShapeDtypeStruct((rows, width), BF16)
    return pl.pallas_call(
        _order_kernel,
        in_specs=[VMEM],
        out_specs=[VMEM] * 2,
        out_shape=[shape, shape],
        compiler_params=pltpu.CompilerParams(vmem_limit_bytes=8 * MIB),
        name="order_rows",
    )(tokens)


def _weight_columns(weights, block, width):
    column = pl.multiple_of(block * width, 128)
    return jnp.concatenate([w[:, pl.ds(column, width)] for w in weights], axis=0)


def _own_kernel(mine, other, g0, g1, u0, u1, out):
    _, _, _, l, c = _place()
    width = mine.shape[1]
    for k, own in enumerate((mine, other)):
        w = _weight_columns((g0, g1, u0, u1), 2 * l + (c if k == 0 else 1 - c), width)
        t = jnp.concatenate([own[:32], own[64:160], own[32:64], own[160:]], axis=0)
        part = lax.dot_general(w, t, NT, preferred_element_type=F32)
        if k == 0:
            out[...] = part
        else:
            out[...] += part


def _own(mine, other, weights):
    units, (rows, width) = weights[0].shape[0], mine.shape
    return pl.pallas_call(
        _own_kernel,
        in_specs=[VMEM] * 6,
        out_specs=VMEM,
        out_shape=jax.ShapeDtypeStruct((4 * units, rows), F32),
        compiler_params=pltpu.CompilerParams(vmem_limit_bytes=16 * MIB),
        cost_estimate=pl.CostEstimate(
            flops=2 * 8 * units * rows * width, bytes_accessed=20 * units * width, transcendentals=0
        ),
        name="own_features",
    )(mine, other, *weights)


def _pack_kernel(p0, p1, p2, first_back, first_on, second_back, second_on):
    for i, piece in enumerate((p0, p1, p2)):
        for j in range(2):
            k = 2 * i + j
            a, b = piece[j, :32], piece[j, 32:]
            first_back[k] = jnp.concatenate([a, b[:16]], axis=0)
            first_on[k] = jnp.concatenate([a, b[16:]], axis=0)
            second_back[k] = jnp.concatenate([a[:16], b], axis=0)
            second_on[k] = jnp.concatenate([a[16:], b], axis=0)


def _pack(pieces):
    send = jax.ShapeDtypeStruct((6, 48, pieces[0].shape[-1]), BF16)
    return pl.pallas_call(
        _pack_kernel,
        in_specs=[VMEM] * 3,
        out_specs=[VMEM] * 4,
        out_shape=[send] * 4,
        compiler_params=pltpu.CompilerParams(vmem_limit_bytes=16 * MIB),
        name="pack_quarters",
    )(*pieces)


def _hidden_kernel(z0, z1, z2, p1, m1, p2, m2, start, g0, g1, u0, u1, out, acc):
    x, y, _, l, c = _place()
    first, second = _along(c, x, y)
    width = z0.shape[-1]
    units = g0.shape[0]
    for k in range(6):
        block = 2 * lax.rem(l + 1 + k // 2, 4) + (c if k % 2 == 0 else 1 - c)
        w = _weight_columns((g0, g1, u0, u1), block, width)
        kept = (z0, z1, z2)[k // 2][k % 2]
        t = jnp.concatenate(
            [
                kept[:32],
                p1[k, :32],
                p2[k, :16],
                m2[k, :16],
                m1[k, :32],
                kept[32:],
                p2[k, 16:],
                p1[k, 32:],
                m1[k, 32:],
                m2[k, 16:],
            ],
            axis=0,
        )
        part = lax.dot_general(w, t, NT, preferred_element_type=F32)
        if k == 0:
            acc[...] = start[...] + part
        else:
            acc[...] += part
    gate = acc[pl.ds(0, 2 * units), :]
    up = acc[pl.ds(2 * units, 2 * units), :]
    hidden = gate / (1 + jnp.exp(-gate)) * up
    half = hidden.shape[1] // 2
    group = half // 4
    turns = (2 * lax.rem(second, 2), lax.rem(first + second, 4))
    for i, turn in enumerate(turns):
        part = pltpu.roll(hidden[:, i * half : (i + 1) * half], turn * group, 1)
        out[:, i * half : (i + 1) * half] = part.astype(BF16)


def _hidden(kept, around, start, weights):
    units, width = weights[0].shape[0], kept[0].shape[-1]
    rows = start.shape[1]
    return pl.pallas_call(
        _hidden_kernel,
        in_specs=[VMEM] * 12,
        out_specs=VMEM,
        out_shape=jax.ShapeDtypeStruct((2 * units, rows), BF16),
        scratch_shapes=[pltpu.VMEM((4 * units, rows), F32)],
        compiler_params=pltpu.CompilerParams(vmem_limit_bytes=24 * MIB),
        cost_estimate=pl.CostEstimate(
            flops=2 * 24 * units * rows * width,
            bytes_accessed=48 * units * width,
            transcendentals=2 * units * rows,
        ),
        name="gate_up_silu",
    )(*kept, *around, start, *weights)


def _down_kernel(h0, h1, h2, h3, d0, d1, own, s1, s2, s3, ht):
    _, _, _, l, c = _place()
    units = h0.shape[0] // 2
    for k, part in enumerate((h0, h1, h2, h3)):
        base = lax.rem(l + k, 4) * (2 * units)
        for i, core in enumerate((c, 1 - c)):
            row = pl.multiple_of(base + core * units, 16)
            ht[pl.ds(row, units), :] = part[pl.ds(i * units, units), :]
    hidden = ht[...].T
    half = hidden.shape[0] // 2
    group = half // 4
    for i, d in enumerate((d0, d1)):
        result = jnp.dot(hidden, d[...], preferred_element_type=F32)
        for k, out in enumerate((own, s1, s2, s3)):
            for j in range(2):
                rows = result[j * half + k * group : j * half + (k + 1) * group]
                out[i, j * group : (j + 1) * group, :] = rows.astype(out.dtype)


def _down(hs, d0, d1):
    rows = hs[0].shape[1]
    depth, width = d0.shape
    block = rows // 4
    send = jax.ShapeDtypeStruct((2, block, width), BF16)
    return pl.pallas_call(
        _down_kernel,
        in_specs=[VMEM] * 6,
        out_specs=[VMEM] * 4,
        out_shape=[jax.ShapeDtypeStruct((2, block, width), F32), send, send, send],
        scratch_shapes=[pltpu.VMEM((depth, rows), BF16)],
        compiler_params=pltpu.CompilerParams(vmem_limit_bytes=24 * MIB),
        cost_estimate=pl.CostEstimate(
            flops=4 * rows * depth * width, bytes_accessed=4 * depth * width, transcendentals=0
        ),
        name="down",
    )(*hs, d0, d1)


def _sum_first_kernel(own, g1, g2, g3, kept, s1, s2, s3):
    x, y, _, _, c = _place()
    _, second = _along(c, x, y)
    for k, out in enumerate((kept, s1, s2, s3)):
        rows = pl.ds(pl.multiple_of(lax.rem(second + k, 4) * 16, 16), 16)
        total = own[:, rows, :]
        for g in (g1, g2, g3):
            total = total + g[:, rows, :].astype(F32)
        out[...] = total.astype(out.dtype)


def _sum_first(own, got):
    width = own.shape[-1]
    send = jax.ShapeDtypeStruct((2, 16, width), BF16)
    return pl.pallas_call(
        _sum_first_kernel,
        in_specs=[VMEM] * 4,
        out_specs=[VMEM] * 4,
        out_shape=[jax.ShapeDtypeStruct((2, 16, width), F32), send, send, send],
        compiler_params=pltpu.CompilerParams(vmem_limit_bytes=8 * MIB),
        name="sum_first",
    )(own, *got)


def _sum_second_kernel(own, g1, g2, g3, here, there):
    _, _, h, _, _ = _place()
    total = own[...]
    for g in (g1, g2, g3):
        total = total + g[...].astype(F32)
    low, high = total[:, :8], total[:, 8:]
    here[...] = jnp.where(h == 0, low, high)
    send = jnp.where(h == 0, high, low)
    there[...] = jnp.concatenate([send[0], send[1]], axis=0).astype(BF16)


def _sum_second(own, got):
    width = own.shape[-1]
    return pl.pallas_call(
        _sum_second_kernel,
        in_specs=[VMEM] * 4,
        out_specs=[VMEM] * 2,
        out_shape=[jax.ShapeDtypeStruct((2, 8, width), F32), jax.ShapeDtypeStruct((16, width), BF16)],
        compiler_params=pltpu.CompilerParams(vmem_limit_bytes=8 * MIB),
        name="sum_second",
    )(own, *got)


def _sum_last_kernel(here, got, own, cross):
    total = got[...].astype(F32)
    own[...] = here[0] + total[:8]
    cross[...] = here[1] + total[8:]


def _sum_last(here, got):
    part = jax.ShapeDtypeStruct((8, got.shape[-1]), F32)
    return pl.pallas_call(
        _sum_last_kernel,
        in_specs=[VMEM] * 2,
        out_specs=[VMEM] * 2,
        out_shape=[part, part],
        compiler_params=pltpu.CompilerParams(vmem_limit_bytes=8 * MIB),
        name="sum_last",
    )(here, got)


def local(tokens, gate_weight, up_weight, down_weight):
    core = lax.axis_index("c")
    mine, theirs = _order(tokens)
    other = _permute(theirs, _swap)
    quarter = jnp.stack([mine[:64], other[:64]])
    kept = [_permute(quarter, m) for m in (_z(-1), _z_two, _z(1))]
    gate_in, up_in, _ = lax.optimization_barrier((gate_weight, up_weight, other))
    gate_other = _permute(gate_in, _swap)
    up_other = _permute(up_in, _swap)
    weights = (gate_weight, gate_other, up_weight, up_other)

    packed = _pack(kept)
    packed, gate_other, up_other = lax.optimization_barrier((packed, gate_other, up_other))
    down_in, _ = lax.optimization_barrier((down_weight, packed))
    down_other = _permute(down_in, _swap)
    first_back, first_on, second_back, second_on = packed
    around = [
        _permute(first_back, _first(-1)),
        _permute(first_on, _first(1)),
        _permute(second_back, _second(-1)),
        _permute(second_on, _second(1)),
    ]
    mine, _ = lax.optimization_barrier((mine, packed))
    start = _own(mine, other, weights)

    hidden = _hidden(kept, around, start, weights)
    two, one, three = (_permute(hidden, _lo(-k)) for k in (2, 1, 3))

    own, *sends = _down((hidden, one, two, three), down_weight, down_other)
    own, *sends = _sum_first(own, [_permute(sends[k - 1], _first(k)) for k in (2, 1, 3)])
    here, there = _sum_second(own, [_permute(sends[k - 1], _second(k)) for k in (2, 1, 3)])
    own, cross = _sum_last(here, _permute(there, _z(4)))
    cross = _permute(cross, _swap)
    mine = lax.broadcasted_iota(jnp.int32, (2, 1, 1), 0) == core
    return jnp.where(mine, own[None], cross[None]).astype(BF16)


def solution(mesh):
    fine = Mesh(mesh.devices.reshape(SIZES), AXES)
    wide, narrow = ("x", "y", "h"), ("l", "c")
    return jax.shard_map(
        local,
        mesh=fine,
        in_specs=(
            P(None, None, narrow),
            P(wide + narrow, None),
            P(wide + narrow, None),
            P(wide, narrow),
        ),
        out_specs=P(None, wide, narrow),
        check_vma=False,
    )
```

```python
import jax
import jax.numpy as jnp
import numpy as np
from jax import lax
from jax.experimental import pallas as pl
from jax.experimental.pallas import tpu as pltpu
from jax.sharding import Mesh, PartitionSpec as P

AXES = ("x", "y", "h", "l", "c")
SIZES = (4, 4, 2, 4, 2)
F32 = jnp.float32
BF16 = jnp.bfloat16
MIB = 1 << 20


def _perm(move):
    pairs = []
    for source in range(256):
        x, y, h, l, c = (int(i) for i in np.unravel_index(source, SIZES))
        X, Y, Z, C = move(x, y, h * 4 + l, c)
        Z %= 8
        pairs.append((source, int(np.ravel_multi_index((X % 4, Y % 4, Z // 4, Z % 4, C % 2), SIZES))))
    return pairs


def _permute(a, move):
    return lax.ppermute(a, AXES, _perm(move))


def _first(k):
    return lambda x, y, z, c: (x + k, y, z, c) if c == 0 else (x, y + k, z, c)


def _second(k):
    return lambda x, y, z, c: (x, y + k, z, c) if c == 0 else (x + k, y, z, c)


def _swap(x, y, z, c):
    return (x, y, z, 1 - c)


def _z(k):
    return lambda x, y, z, c: (x, y, z + k, c)


def _up_or_down(k):
    return lambda x, y, z, c: (x, y, z + k if c == 0 else z - k, c)


def _z_two(x, y, z, c):
    return (x, y, z + 2 if z % 2 == 0 else z - 2, c)


def _lo(k):
    return lambda x, y, z, c: (x, y, (z // 4) * 4 + (z % 4 + k) % 4, c)


def _only(core, move):
    return [(s, d) for s, d in _perm(move) if s % 2 == core]


VMEM = pl.BlockSpec(memory_space=pltpu.VMEM)
NT = (((1,), (1,)), ((), ()))


def _place():
    return [lax.axis_index(a).astype(jnp.int32) for a in AXES]


def _along(core, x, y):
    return jnp.where(core == 0, x, y), jnp.where(core == 0, y, x)


def _order_kernel(tokens, mine, theirs):
    x, y, _, _, c = _place()
    for core, out in ((c, mine), (1 - c, theirs)):
        first, second = _along(core, x, y)
        for half, q in enumerate((first + 2 * second, 2 * first + second)):
            for i in range(4):
                a = lax.rem(q + i, 4)
                base = 64 + half * 96 + (i - 1) * 32 if i else half * 32
                for j in range(2):
                    b = 2 * half + j
                    block = jnp.where(core == 0, a * 4 + b, b * 4 + a)
                    row = pl.multiple_of(block * 16, 16)
                    out[pl.ds(base + j * 16, 16), :] = tokens[core, pl.ds(row, 16), :]


def _order(tokens):
    _, rows, width = tokens.shape
    shape = jax.ShapeDtypeStruct((rows, width), BF16)
    return pl.pallas_call(
        _order_kernel,
        in_specs=[VMEM],
        out_specs=[VMEM] * 2,
        out_shape=[shape, shape],
        compiler_params=pltpu.CompilerParams(vmem_limit_bytes=8 * MIB),
        name="order_rows",
    )(tokens)


def _weight_columns(weights, block, width):
    column = pl.multiple_of(block * width, 128)
    return jnp.concatenate([w[:, pl.ds(column, width)] for w in weights], axis=0)


def _in_order(rows):
    return jnp.concatenate([rows[:32], rows[64:160], rows[32:64], rows[160:]], axis=0)


def _own_kernel(mine, other, g0, g1, u0, u1, out):
    _, _, _, l, c = _place()
    width = mine.shape[1]
    for k, own in enumerate((mine, other)):
        w = _weight_columns((g0, g1, u0, u1), 2 * l + (c if k == 0 else 1 - c), width)
        part = lax.dot_general(w, _in_order(own), NT, preferred_element_type=F32)
        if k == 0:
            out[...] = part
        else:
            out[...] += part


def _own(mine, other, weights):
    units, (rows, width) = weights[0].shape[0], mine.shape
    return pl.pallas_call(
        _own_kernel,
        in_specs=[VMEM] * 6,
        out_specs=VMEM,
        out_shape=jax.ShapeDtypeStruct((4 * units, rows), F32),
        compiler_params=pltpu.CompilerParams(vmem_limit_bytes=16 * MIB),
        cost_estimate=pl.CostEstimate(
            flops=2 * 8 * units * rows * width, bytes_accessed=20 * units * width, transcendentals=0
        ),
        name="own_features",
    )(mine, other, *weights)


def _pack_kernel(near, two, first_back, first_on, second_back, second_on):
    for i, piece in enumerate((near, two)):
        for j in range(2):
            k = 2 * i + j
            a, b = piece[j, :32], piece[j, 32:]
            first_back[k] = jnp.concatenate([a, b[:16]], axis=0)
            first_on[k] = jnp.concatenate([a, b[16:]], axis=0)
            second_back[k] = jnp.concatenate([a[:16], b], axis=0)
            second_on[k] = jnp.concatenate([a[16:], b], axis=0)


def _pack(pieces):
    send = jax.ShapeDtypeStruct((4, 48, pieces[0].shape[-1]), BF16)
    return pl.pallas_call(
        _pack_kernel,
        in_specs=[VMEM] * 2,
        out_specs=[VMEM] * 4,
        out_shape=[send] * 4,
        compiler_params=pltpu.CompilerParams(vmem_limit_bytes=16 * MIB),
        name="pack_quarters",
    )(*pieces)


def _hidden_kernel(near, two, p1, m1, p2, m2, direct, start, g0, g1, u0, u1, out, acc):
    x, y, _, l, c = _place()
    first, second = _along(c, x, y)
    width = near.shape[-1]
    units = g0.shape[0]
    ahead = (jnp.where(c == 0, 3, 1), 2, jnp.where(c == 0, 1, 3))
    for k in range(6):
        block = 2 * lax.rem(l + ahead[k // 2], 4) + (c if k % 2 == 0 else 1 - c)
        w = _weight_columns((g0, g1, u0, u1), block, width)
        if k < 4:
            kept = (near, two)[k // 2][k % 2]
            t = jnp.concatenate(
                [
                    kept[:32],
                    p1[k, :32],
                    p2[k, :16],
                    m2[k, :16],
                    m1[k, :32],
                    kept[32:],
                    p2[k, 16:],
                    p1[k, 32:],
                    m1[k, 32:],
                    m2[k, 16:],
                ],
                axis=0,
            )
        else:
            t = _in_order(direct[k - 4])
        part = lax.dot_general(w, t, NT, preferred_element_type=F32)
        if k == 0:
            acc[...] = start[...] + part
        else:
            acc[...] += part
    gate = acc[pl.ds(0, 2 * units), :]
    up = acc[pl.ds(2 * units, 2 * units), :]
    hidden = gate / (1 + jnp.exp(-gate)) * up
    half = hidden.shape[1] // 2
    group = half // 4
    turns = (2 * lax.rem(second, 2), lax.rem(first + second, 4))
    for i, turn in enumerate(turns):
        part = pltpu.roll(hidden[:, i * half : (i + 1) * half], turn * group, 1)
        out[:, i * half : (i + 1) * half] = part.astype(BF16)


def _hidden(kept, around, direct, start, weights):
    units, width = weights[0].shape[0], kept[0].shape[-1]
    rows = start.shape[1]
    return pl.pallas_call(
        _hidden_kernel,
        in_specs=[VMEM] * 12,
        out_specs=VMEM,
        out_shape=jax.ShapeDtypeStruct((2 * units, rows), BF16),
        scratch_shapes=[pltpu.VMEM((4 * units, rows), F32)],
        compiler_params=pltpu.CompilerParams(vmem_limit_bytes=24 * MIB),
        cost_estimate=pl.CostEstimate(
            flops=2 * 24 * units * rows * width,
            bytes_accessed=48 * units * width,
            transcendentals=2 * units * rows,
        ),
        name="gate_up_silu",
    )(*kept, *around, direct, start, *weights)


def _down_kernel(h0, h1, h2, h3, d0, d1, own, s1, s2, s3, ht):
    _, _, _, l, c = _place()
    units = h0.shape[0] // 2
    for k, part in enumerate((h0, h1, h2, h3)):
        base = lax.rem(l + k, 4) * (2 * units)
        for i, core in enumerate((c, 1 - c)):
            row = pl.multiple_of(base + core * units, 16)
            ht[pl.ds(row, units), :] = part[pl.ds(i * units, units), :]
    hidden = ht[...].T
    half = hidden.shape[0] // 2
    group = half // 4
    for i, d in enumerate((d0, d1)):
        result = jnp.dot(hidden, d[...], preferred_element_type=F32)
        for k, out in enumerate((own, s1, s2, s3)):
            for j in range(2):
                rows = result[j * half + k * group : j * half + (k + 1) * group]
                out[i, j * group : (j + 1) * group, :] = rows.astype(out.dtype)


def _down(hs, d0, d1):
    rows = hs[0].shape[1]
    depth, width = d0.shape
    block = rows // 4
    send = jax.ShapeDtypeStruct((2, block, width), BF16)
    return pl.pallas_call(
        _down_kernel,
        in_specs=[VMEM] * 6,
        out_specs=[VMEM] * 4,
        out_shape=[jax.ShapeDtypeStruct((2, block, width), F32), send, send, send],
        scratch_shapes=[pltpu.VMEM((depth, rows), BF16)],
        compiler_params=pltpu.CompilerParams(vmem_limit_bytes=24 * MIB),
        cost_estimate=pl.CostEstimate(
            flops=4 * rows * depth * width, bytes_accessed=4 * depth * width, transcendentals=0
        ),
        name="down",
    )(*hs, d0, d1)


def _sum_first_kernel(own, g1, g2, g3, kept, s1, s2, s3):
    x, y, _, _, c = _place()
    _, second = _along(c, x, y)
    for k, out in enumerate((kept, s1, s2, s3)):
        rows = pl.ds(pl.multiple_of(lax.rem(second + k, 4) * 16, 16), 16)
        total = own[:, rows, :]
        for g in (g1, g2, g3):
            total = total + g[:, rows, :].astype(F32)
        out[...] = total.astype(out.dtype)


def _sum_first(own, got):
    width = own.shape[-1]
    send = jax.ShapeDtypeStruct((2, 16, width), BF16)
    return pl.pallas_call(
        _sum_first_kernel,
        in_specs=[VMEM] * 4,
        out_specs=[VMEM] * 4,
        out_shape=[jax.ShapeDtypeStruct((2, 16, width), F32), send, send, send],
        compiler_params=pltpu.CompilerParams(vmem_limit_bytes=8 * MIB),
        name="sum_first",
    )(own, *got)


def _sum_second_kernel(own, g1, g2, g3, here, there):
    _, _, h, _, _ = _place()
    total = own[...]
    for g in (g1, g2, g3):
        total = total + g[...].astype(F32)
    low, high = total[:, :8], total[:, 8:]
    here[...] = jnp.where(h == 0, low, high)
    send = jnp.where(h == 0, high, low)
    there[...] = jnp.concatenate([send[0], send[1]], axis=0).astype(BF16)


def _sum_second(own, got):
    width = own.shape[-1]
    return pl.pallas_call(
        _sum_second_kernel,
        in_specs=[VMEM] * 4,
        out_specs=[VMEM] * 2,
        out_shape=[jax.ShapeDtypeStruct((2, 8, width), F32), jax.ShapeDtypeStruct((16, width), BF16)],
        compiler_params=pltpu.CompilerParams(vmem_limit_bytes=8 * MIB),
        name="sum_second",
    )(own, *got)


def _sum_last_kernel(here, got, own, cross):
    total = got[...].astype(F32)
    own[...] = here[0] + total[:8]
    cross[...] = here[1] + total[8:]


def _sum_last(here, got):
    part = jax.ShapeDtypeStruct((8, got.shape[-1]), F32)
    return pl.pallas_call(
        _sum_last_kernel,
        in_specs=[VMEM] * 2,
        out_specs=[VMEM] * 2,
        out_shape=[part, part],
        compiler_params=pltpu.CompilerParams(vmem_limit_bytes=8 * MIB),
        name="sum_last",
    )(here, got)


def local(tokens, gate_weight, up_weight, down_weight):
    core = lax.axis_index("c")
    mine, theirs = _order(tokens)
    other = _permute(theirs, _swap)
    quarter = jnp.stack([mine[:64], other[:64]])
    near = _permute(quarter, _up_or_down(1))
    two = _permute(quarter, _z_two)
    gate_in, up_in, _ = lax.optimization_barrier((gate_weight, up_weight, other))
    gate_other = _permute(gate_in, _swap)
    up_other = _permute(up_in, _swap)
    weights = (gate_weight, gate_other, up_weight, up_other)
    whole, near, two = lax.optimization_barrier((jnp.stack([mine, other]), near, two))
    direct = _permute(whole, _up_or_down(-1))

    packed = _pack((near, two))
    packed, gate_other, up_other = lax.optimization_barrier((packed, gate_other, up_other))
    first_back, first_on, second_back, second_on = packed
    around = [
        _permute(first_back, _first(-1)),
        _permute(first_on, _first(1)),
        _permute(second_back, _second(-1)),
        _permute(second_on, _second(1)),
    ]
    mine, _ = lax.optimization_barrier((mine, packed))
    start = _own(mine, other, weights)

    hidden = _hidden((near, two), around, direct, start, weights)
    down_in, _ = lax.optimization_barrier((down_weight, hidden))
    down_other = _permute(down_in, _swap)
    two, one, three = (_permute(hidden, _lo(-k)) for k in (2, 1, 3))

    own, *sends = _down((hidden, one, two, three), down_weight, down_other)
    own, *sends = _sum_first(own, [_permute(sends[k - 1], _first(k)) for k in (2, 1, 3)])
    here, there = _sum_second(own, [_permute(sends[k - 1], _second(k)) for k in (2, 1, 3)])
    own, cross = _sum_last(here, _permute(there, _z(4)))
    cross = _permute(cross, _swap)
    mine = lax.broadcasted_iota(jnp.int32, (2, 1, 1), 0) == core
    return jnp.where(mine, own[None], cross[None]).astype(BF16)


def solution(mesh):
    fine = Mesh(mesh.devices.reshape(SIZES), AXES)
    wide, narrow = ("x", "y", "h"), ("l", "c")
    return jax.shard_map(
        local,
        mesh=fine,
        in_specs=(
            P(None, None, narrow),
            P(wide + narrow, None),
            P(wide + narrow, None),
            P(wide, narrow),
        ),
        out_specs=P(None, wide, narrow),
        check_vma=False,
    )
```

```python
import jax
import jax.numpy as jnp
import numpy as np
from jax import lax
from jax.experimental import pallas as pl
from jax.experimental.pallas import tpu as pltpu
from jax.sharding import Mesh, PartitionSpec as P

AXES = ("x", "y", "h", "l", "c")
SIZES = (4, 4, 2, 4, 2)
F32 = jnp.float32
BF16 = jnp.bfloat16
MIB = 1 << 20


def _perm(move):
    pairs = []
    for source in range(256):
        x, y, h, l, c = (int(i) for i in np.unravel_index(source, SIZES))
        X, Y, Z, C = move(x, y, h * 4 + l, c)
        Z %= 8
        pairs.append((source, int(np.ravel_multi_index((X % 4, Y % 4, Z // 4, Z % 4, C % 2), SIZES))))
    return pairs


def _permute(a, move):
    return lax.ppermute(a, AXES, _perm(move))


def _first(k):
    return lambda x, y, z, c: (x + k, y, z, c) if c == 0 else (x, y + k, z, c)


def _second(k):
    return lambda x, y, z, c: (x, y + k, z, c) if c == 0 else (x + k, y, z, c)


def _swap(x, y, z, c):
    return (x, y, z, 1 - c)


def _z(k):
    return lambda x, y, z, c: (x, y, z + k, c)


def _up_or_down(k):
    return lambda x, y, z, c: (x, y, z + k if c == 0 else z - k, c)


def _z_two(x, y, z, c):
    return (x, y, z + 2 if z % 2 == 0 else z - 2, c)


def _lo(k):
    return lambda x, y, z, c: (x, y, (z // 4) * 4 + (z % 4 + k) % 4, c)


def _only(core, move):
    return [(s, d) for s, d in _perm(move) if s % 2 == core]


VMEM = pl.BlockSpec(memory_space=pltpu.VMEM)
NT = (((1,), (1,)), ((), ()))


def _place():
    return [lax.axis_index(a).astype(jnp.int32) for a in AXES]


def _along(core, x, y):
    return jnp.where(core == 0, x, y), jnp.where(core == 0, y, x)


def _order(tokens, out):
    x, y, _, _, c = _place()
    first, second = _along(c, x, y)
    for half, q in enumerate((first + 2 * second, 2 * first + second)):
        for i in range(4):
            a = lax.rem(q + i, 4)
            base = 64 + half * 96 + (i - 1) * 32 if i else half * 32
            for j in range(2):
                b = 2 * half + j
                block = jnp.where(c == 0, a * 4 + b, b * 4 + a)
                row = pl.multiple_of(block * 16, 16)
                out[pl.ds(base + j * 16, 16), :] = tokens[c, pl.ds(row, 16), :]


def _mine_kernel(tokens, mine):
    _order(tokens, mine)


def _mine(tokens):
    _, rows, width = tokens.shape
    return pl.pallas_call(
        _mine_kernel,
        in_specs=[VMEM],
        out_specs=VMEM,
        out_shape=jax.ShapeDtypeStruct((rows, width), BF16),
        compiler_params=pltpu.CompilerParams(vmem_limit_bytes=8 * MIB),
        name="order_own",
    )(tokens)


def _join_kernel(mine, swapped, quarter, whole):
    lead = quarter.shape[1]
    whole[0] = mine[...]
    _order(swapped, whole.at[1])
    quarter[0] = mine[:lead]
    quarter[1] = whole[1, :lead]


def _join(mine, swapped):
    rows, width = mine.shape
    return pl.pallas_call(
        _join_kernel,
        in_specs=[VMEM] * 2,
        out_specs=[VMEM] * 2,
        out_shape=[
            jax.ShapeDtypeStruct((2, rows // 4, width), BF16),
            jax.ShapeDtypeStruct((2, rows, width), BF16),
        ],
        compiler_params=pltpu.CompilerParams(vmem_limit_bytes=8 * MIB),
        name="order_other",
    )(mine, swapped)


def _weight_columns(weights, block, width):
    column = pl.multiple_of(block * width, 128)
    return jnp.concatenate([w[:, pl.ds(column, width)] for w in weights], axis=0)


def _in_order(rows):
    return jnp.concatenate([rows[:32], rows[64:160], rows[32:64], rows[160:]], axis=0)


def _own_kernel(whole, g0, g1, u0, u1, out):
    _, _, _, l, c = _place()
    width = whole.shape[-1]
    for k in range(2):
        w = _weight_columns((g0, g1, u0, u1), 2 * l + (c if k == 0 else 1 - c), width)
        part = lax.dot_general(w, _in_order(whole[k]), NT, preferred_element_type=F32)
        if k == 0:
            out[...] = part
        else:
            out[...] += part


def _own(whole, weights):
    units, (_, rows, width) = weights[0].shape[0], whole.shape
    return pl.pallas_call(
        _own_kernel,
        in_specs=[VMEM] * 5,
        out_specs=VMEM,
        out_shape=jax.ShapeDtypeStruct((4 * units, rows), F32),
        compiler_params=pltpu.CompilerParams(vmem_limit_bytes=16 * MIB),
        cost_estimate=pl.CostEstimate(
            flops=2 * 8 * units * rows * width, bytes_accessed=20 * units * width, transcendentals=0
        ),
        name="own_features",
    )(whole, *weights)


def _pack_kernel(near, two, first_back, first_on, second_back, second_on):
    for i, piece in enumerate((near, two)):
        for j in range(2):
            k = 2 * i + j
            a, b = piece[j, :32], piece[j, 32:]
            first_back[k] = jnp.concatenate([a, b[:16]], axis=0)
            first_on[k] = jnp.concatenate([a, b[16:]], axis=0)
            second_back[k] = jnp.concatenate([a[:16], b], axis=0)
            second_on[k] = jnp.concatenate([a[16:], b], axis=0)


def _pack(pieces):
    send = jax.ShapeDtypeStruct((4, 48, pieces[0].shape[-1]), BF16)
    return pl.pallas_call(
        _pack_kernel,
        in_specs=[VMEM] * 2,
        out_specs=[VMEM] * 4,
        out_shape=[send] * 4,
        compiler_params=pltpu.CompilerParams(vmem_limit_bytes=16 * MIB),
        name="pack_quarters",
    )(*pieces)


def _hidden_kernel(near, two, p1, m1, p2, m2, direct, start, g0, g1, u0, u1, out, acc):
    x, y, _, l, c = _place()
    first, second = _along(c, x, y)
    width = near.shape[-1]
    units = g0.shape[0]
    ahead = (jnp.where(c == 0, 3, 1), 2, jnp.where(c == 0, 1, 3))
    for k in range(6):
        block = 2 * lax.rem(l + ahead[k // 2], 4) + (c if k % 2 == 0 else 1 - c)
        w = _weight_columns((g0, g1, u0, u1), block, width)
        if k < 4:
            kept = (near, two)[k // 2][k % 2]
            t = jnp.concatenate(
                [
                    kept[:32],
                    p1[k, :32],
                    p2[k, :16],
                    m2[k, :16],
                    m1[k, :32],
                    kept[32:],
                    p2[k, 16:],
                    p1[k, 32:],
                    m1[k, 32:],
                    m2[k, 16:],
                ],
                axis=0,
            )
        else:
            t = _in_order(direct[k - 4])
        part = lax.dot_general(w, t, NT, preferred_element_type=F32)
        if k == 0:
            acc[...] = start[...] + part
        else:
            acc[...] += part
    gate = acc[pl.ds(0, 2 * units), :]
    up = acc[pl.ds(2 * units, 2 * units), :]
    hidden = gate / (1 + jnp.exp(-gate)) * up
    half = hidden.shape[1] // 2
    group = half // 4
    turns = (2 * lax.rem(second, 2), lax.rem(first + second, 4))
    for i, turn in enumerate(turns):
        part = pltpu.roll(hidden[:, i * half : (i + 1) * half], turn * group, 1)
        out[:, i * half : (i + 1) * half] = part.astype(BF16)


def _hidden(kept, around, direct, start, weights):
    units, width = weights[0].shape[0], kept[0].shape[-1]
    rows = start.shape[1]
    return pl.pallas_call(
        _hidden_kernel,
        in_specs=[VMEM] * 12,
        out_specs=VMEM,
        out_shape=jax.ShapeDtypeStruct((2 * units, rows), BF16),
        scratch_shapes=[pltpu.VMEM((4 * units, rows), F32)],
        compiler_params=pltpu.CompilerParams(vmem_limit_bytes=24 * MIB),
        cost_estimate=pl.CostEstimate(
            flops=2 * 24 * units * rows * width,
            bytes_accessed=48 * units * width,
            transcendentals=2 * units * rows,
        ),
        name="gate_up_silu",
    )(*kept, *around, direct, start, *weights)


def _down_kernel(h0, h1, h2, h3, d0, d1, own, s1, s2, s3, ht):
    _, _, _, l, c = _place()
    units = h0.shape[0] // 2
    for k, part in enumerate((h0, h1, h2, h3)):
        base = lax.rem(l + k, 4) * (2 * units)
        for i, core in enumerate((c, 1 - c)):
            row = pl.multiple_of(base + core * units, 16)
            ht[pl.ds(row, units), :] = part[pl.ds(i * units, units), :]
    hidden = ht[...].T
    half = hidden.shape[0] // 2
    group = half // 4
    for i, d in enumerate((d0, d1)):
        result = jnp.dot(hidden, d[...], preferred_element_type=F32)
        for k, out in enumerate((own, s1, s2, s3)):
            for j in range(2):
                rows = result[j * half + k * group : j * half + (k + 1) * group]
                out[i, j * group : (j + 1) * group, :] = rows.astype(out.dtype)


def _down(hs, d0, d1):
    rows = hs[0].shape[1]
    depth, width = d0.shape
    block = rows // 4
    send = jax.ShapeDtypeStruct((2, block, width), BF16)
    return pl.pallas_call(
        _down_kernel,
        in_specs=[VMEM] * 6,
        out_specs=[VMEM] * 4,
        out_shape=[jax.ShapeDtypeStruct((2, block, width), F32), send, send, send],
        scratch_shapes=[pltpu.VMEM((depth, rows), BF16)],
        compiler_params=pltpu.CompilerParams(vmem_limit_bytes=24 * MIB),
        cost_estimate=pl.CostEstimate(
            flops=4 * rows * depth * width, bytes_accessed=4 * depth * width, transcendentals=0
        ),
        name="down",
    )(*hs, d0, d1)


def _sum_first_kernel(own, g1, g2, g3, kept, s1, s2, s3):
    x, y, _, _, c = _place()
    _, second = _along(c, x, y)
    for k, out in enumerate((kept, s1, s2, s3)):
        rows = pl.ds(pl.multiple_of(lax.rem(second + k, 4) * 16, 16), 16)
        total = own[:, rows, :]
        for g in (g1, g2, g3):
            total = total + g[:, rows, :].astype(F32)
        out[...] = total.astype(out.dtype)


def _sum_first(own, got):
    width = own.shape[-1]
    send = jax.ShapeDtypeStruct((2, 16, width), BF16)
    return pl.pallas_call(
        _sum_first_kernel,
        in_specs=[VMEM] * 4,
        out_specs=[VMEM] * 4,
        out_shape=[jax.ShapeDtypeStruct((2, 16, width), F32), send, send, send],
        compiler_params=pltpu.CompilerParams(vmem_limit_bytes=8 * MIB),
        name="sum_first",
    )(own, *got)


def _sum_second_kernel(own, g1, g2, g3, here, there):
    _, _, h, _, _ = _place()
    total = own[...]
    for g in (g1, g2, g3):
        total = total + g[...].astype(F32)
    low, high = total[:, :8], total[:, 8:]
    here[...] = jnp.where(h == 0, low, high)
    send = jnp.where(h == 0, high, low)
    there[...] = jnp.concatenate([send[0], send[1]], axis=0).astype(BF16)


def _sum_second(own, got):
    width = own.shape[-1]
    return pl.pallas_call(
        _sum_second_kernel,
        in_specs=[VMEM] * 4,
        out_specs=[VMEM] * 2,
        out_shape=[jax.ShapeDtypeStruct((2, 8, width), F32), jax.ShapeDtypeStruct((16, width), BF16)],
        compiler_params=pltpu.CompilerParams(vmem_limit_bytes=8 * MIB),
        name="sum_second",
    )(own, *got)


def _sum_last_kernel(here, got, own, cross):
    total = got[...].astype(F32)
    own[...] = here[0] + total[:8]
    cross[...] = here[1] + total[8:]


def _sum_last(here, got):
    part = jax.ShapeDtypeStruct((8, got.shape[-1]), F32)
    return pl.pallas_call(
        _sum_last_kernel,
        in_specs=[VMEM] * 2,
        out_specs=[VMEM] * 2,
        out_shape=[part, part],
        compiler_params=pltpu.CompilerParams(vmem_limit_bytes=8 * MIB),
        name="sum_last",
    )(here, got)


def local(tokens, gate_weight, up_weight, down_weight):
    core = lax.axis_index("c")
    swapped = _permute(tokens, _swap)
    quarter, whole = _join(_mine(tokens), swapped)
    near = _permute(quarter, _up_or_down(1))
    two = _permute(quarter, _z_two)
    gate_in, up_in, _ = lax.optimization_barrier((gate_weight, up_weight, quarter))
    gate_other = _permute(gate_in, _swap)
    up_other = _permute(up_in, _swap)
    weights = (gate_weight, gate_other, up_weight, up_other)
    later, near, two = lax.optimization_barrier((whole, near, two))
    direct = _permute(later, _up_or_down(-1))

    packed = _pack((near, two))
    packed, gate_other, up_other = lax.optimization_barrier((packed, gate_other, up_other))
    first_back, first_on, second_back, second_on = packed
    around = [
        _permute(first_back, _first(-1)),
        _permute(first_on, _first(1)),
        _permute(second_back, _second(-1)),
        _permute(second_on, _second(1)),
    ]
    whole, _ = lax.optimization_barrier((whole, packed))
    start = _own(whole, weights)

    hidden = _hidden((near, two), around, direct, start, weights)
    down_in, _ = lax.optimization_barrier((down_weight, hidden))
    down_other = _permute(down_in, _swap)
    two, one, three = (_permute(hidden, _lo(-k)) for k in (2, 1, 3))

    own, *sends = _down((hidden, one, two, three), down_weight, down_other)
    own, *sends = _sum_first(own, [_permute(sends[k - 1], _first(k)) for k in (2, 1, 3)])
    here, there = _sum_second(own, [_permute(sends[k - 1], _second(k)) for k in (2, 1, 3)])
    own, cross = _sum_last(here, _permute(there, _z(4)))
    cross = _permute(cross, _swap)
    mine = lax.broadcasted_iota(jnp.int32, (2, 1, 1), 0) == core
    return jnp.where(mine, own[None], cross[None]).astype(BF16)


def solution(mesh):
    fine = Mesh(mesh.devices.reshape(SIZES), AXES)
    wide, narrow = ("x", "y", "h"), ("l", "c")
    return jax.shard_map(
        local,
        mesh=fine,
        in_specs=(
            P(None, None, narrow),
            P(wide + narrow, None),
            P(wide + narrow, None),
            P(wide, narrow),
        ),
        out_specs=P(None, wide, narrow),
        check_vma=False,
    )
```

```python
import jax
import jax.numpy as jnp
import numpy as np
from jax import lax
from jax.experimental import pallas as pl
from jax.experimental.pallas import tpu as pltpu
from jax.sharding import Mesh, PartitionSpec as P

AXES = ("x", "y", "h", "l", "c")
SIZES = (4, 4, 2, 4, 2)
F32 = jnp.float32
BF16 = jnp.bfloat16
MIB = 1 << 20


def _perm(move):
    pairs = []
    for source in range(256):
        x, y, h, l, c = (int(i) for i in np.unravel_index(source, SIZES))
        X, Y, Z, C = move(x, y, h * 4 + l, c)
        Z %= 8
        pairs.append((source, int(np.ravel_multi_index((X % 4, Y % 4, Z // 4, Z % 4, C % 2), SIZES))))
    return pairs


def _permute(a, move):
    return lax.ppermute(a, AXES, _perm(move))


def _first(k):
    return lambda x, y, z, c: (x + k, y, z, c) if c == 0 else (x, y + k, z, c)


def _second(k):
    return lambda x, y, z, c: (x, y + k, z, c) if c == 0 else (x + k, y, z, c)


def _swap(x, y, z, c):
    return (x, y, z, 1 - c)


def _z(k):
    return lambda x, y, z, c: (x, y, z + k, c)


def _up_or_down(k):
    return lambda x, y, z, c: (x, y, z + k if c == 0 else z - k, c)


def _z_two(x, y, z, c):
    return (x, y, z + 2 if z % 2 == 0 else z - 2, c)


def _lo(k):
    return lambda x, y, z, c: (x, y, (z // 4) * 4 + (z % 4 + k) % 4, c)


def _only(core, move):
    return [(s, d) for s, d in _perm(move) if s % 2 == core]


VMEM = pl.BlockSpec(memory_space=pltpu.VMEM)
NT = (((1,), (1,)), ((), ()))


def _place():
    return [lax.axis_index(a).astype(jnp.int32) for a in AXES]


def _along(core, x, y):
    return jnp.where(core == 0, x, y), jnp.where(core == 0, y, x)


def _order(tokens, out):
    x, y, _, _, c = _place()
    first, second = _along(c, x, y)
    for half, q in enumerate((first + 2 * second, 2 * first + second)):
        for i in range(4):
            a = lax.rem(q + i, 4)
            base = 64 + half * 96 + (i - 1) * 32 if i else half * 32
            for j in range(2):
                b = 2 * half + j
                block = jnp.where(c == 0, a * 4 + b, b * 4 + a)
                row = pl.multiple_of(block * 16, 16)
                out[pl.ds(base + j * 16, 16), :] = tokens[c, pl.ds(row, 16), :]


def _mine_kernel(tokens, mine):
    _order(tokens, mine)


def _mine(tokens):
    _, rows, width = tokens.shape
    return pl.pallas_call(
        _mine_kernel,
        in_specs=[VMEM],
        out_specs=VMEM,
        out_shape=jax.ShapeDtypeStruct((rows, width), BF16),
        compiler_params=pltpu.CompilerParams(vmem_limit_bytes=8 * MIB),
        name="order_own",
    )(tokens)


def _join_kernel(mine, swapped, quarter, whole):
    lead = quarter.shape[1]
    whole[0] = mine[...]
    _order(swapped, whole.at[1])
    quarter[0] = mine[:lead]
    quarter[1] = whole[1, :lead]


def _join(mine, swapped):
    rows, width = mine.shape
    return pl.pallas_call(
        _join_kernel,
        in_specs=[VMEM] * 2,
        out_specs=[VMEM] * 2,
        out_shape=[
            jax.ShapeDtypeStruct((2, rows // 4, width), BF16),
            jax.ShapeDtypeStruct((2, rows, width), BF16),
        ],
        compiler_params=pltpu.CompilerParams(vmem_limit_bytes=8 * MIB),
        name="order_other",
    )(mine, swapped)


def _weight_columns(weights, block, width):
    column = pl.multiple_of(block * width, 128)
    return jnp.concatenate([w[:, pl.ds(column, width)] for w in weights], axis=0)


def _in_order(rows):
    return jnp.concatenate([rows[:32], rows[64:160], rows[32:64], rows[160:]], axis=0)


def _own_kernel(whole, g0, g1, u0, u1, out):
    _, _, _, l, c = _place()
    width = whole.shape[-1]
    for k in range(2):
        w = _weight_columns((g0, g1, u0, u1), 2 * l + (c if k == 0 else 1 - c), width)
        part = lax.dot_general(w, _in_order(whole[k]), NT, preferred_element_type=F32)
        if k == 0:
            out[...] = part
        else:
            out[...] += part


def _own(whole, weights):
    units, (_, rows, width) = weights[0].shape[0], whole.shape
    return pl.pallas_call(
        _own_kernel,
        in_specs=[VMEM] * 5,
        out_specs=VMEM,
        out_shape=jax.ShapeDtypeStruct((4 * units, rows), F32),
        compiler_params=pltpu.CompilerParams(vmem_limit_bytes=16 * MIB),
        cost_estimate=pl.CostEstimate(
            flops=2 * 8 * units * rows * width, bytes_accessed=20 * units * width, transcendentals=0
        ),
        name="own_features",
    )(whole, *weights)


def _pack_kernel(near, two, first_back, first_on, second_back, second_on):
    for i, piece in enumerate((near, two)):
        for j in range(2):
            k = 2 * i + j
            a, b = piece[j, :32], piece[j, 32:]
            first_back[k] = jnp.concatenate([a, b[:16]], axis=0)
            first_on[k] = jnp.concatenate([a, b[16:]], axis=0)
            second_back[k] = jnp.concatenate([a[:16], b], axis=0)
            second_on[k] = jnp.concatenate([a[16:], b], axis=0)


def _pack(pieces):
    send = jax.ShapeDtypeStruct((4, 48, pieces[0].shape[-1]), BF16)
    return pl.pallas_call(
        _pack_kernel,
        in_specs=[VMEM] * 2,
        out_specs=[VMEM] * 4,
        out_shape=[send] * 4,
        compiler_params=pltpu.CompilerParams(vmem_limit_bytes=16 * MIB),
        name="pack_quarters",
    )(*pieces)


def _around_kernel(near, two, p1, m1, p2, m2, start, g0, g1, u0, u1, out):
    _, _, _, l, c = _place()
    width = near.shape[-1]
    ahead = (jnp.where(c == 0, 3, 1), 2)
    for k in range(4):
        block = 2 * lax.rem(l + ahead[k // 2], 4) + (c if k % 2 == 0 else 1 - c)
        w = _weight_columns((g0, g1, u0, u1), block, width)
        kept = (near, two)[k // 2][k % 2]
        t = jnp.concatenate(
            [
                kept[:32],
                p1[k, :32],
                p2[k, :16],
                m2[k, :16],
                m1[k, :32],
                kept[32:],
                p2[k, 16:],
                p1[k, 32:],
                m1[k, 32:],
                m2[k, 16:],
            ],
            axis=0,
        )
        part = lax.dot_general(w, t, NT, preferred_element_type=F32)
        if k == 0:
            out[...] = start[...] + part
        else:
            out[...] += part


def _around(kept, around, start, weights):
    units, width = weights[0].shape[0], kept[0].shape[-1]
    rows = start.shape[1]
    return pl.pallas_call(
        _around_kernel,
        in_specs=[VMEM] * 11,
        out_specs=VMEM,
        out_shape=jax.ShapeDtypeStruct(start.shape, F32),
        compiler_params=pltpu.CompilerParams(vmem_limit_bytes=16 * MIB),
        cost_estimate=pl.CostEstimate(
            flops=2 * 16 * units * rows * width, bytes_accessed=32 * units * width, transcendentals=0
        ),
        name="gate_up_around",
    )(*kept, *around, start, *weights)


def _hidden_kernel(direct, start, g0, g1, u0, u1, out, acc):
    x, y, _, l, c = _place()
    first, second = _along(c, x, y)
    width = direct.shape[-1]
    units = g0.shape[0]
    for k in range(2):
        block = 2 * lax.rem(l + jnp.where(c == 0, 1, 3), 4) + (c if k == 0 else 1 - c)
        w = _weight_columns((g0, g1, u0, u1), block, width)
        part = lax.dot_general(w, _in_order(direct[k]), NT, preferred_element_type=F32)
        if k == 0:
            acc[...] = start[...] + part
        else:
            acc[...] += part
    gate = acc[pl.ds(0, 2 * units), :]
    up = acc[pl.ds(2 * units, 2 * units), :]
    hidden = gate / (1 + jnp.exp(-gate)) * up
    half = hidden.shape[1] // 2
    group = half // 4
    turns = (2 * lax.rem(second, 2), lax.rem(first + second, 4))
    for i, turn in enumerate(turns):
        part = pltpu.roll(hidden[:, i * half : (i + 1) * half], turn * group, 1)
        out[:, i * half : (i + 1) * half] = part.astype(BF16)


def _hidden(direct, start, weights):
    units, (_, rows, width) = weights[0].shape[0], direct.shape
    return pl.pallas_call(
        _hidden_kernel,
        in_specs=[VMEM] * 6,
        out_specs=VMEM,
        out_shape=jax.ShapeDtypeStruct((2 * units, rows), BF16),
        scratch_shapes=[pltpu.VMEM((4 * units, rows), F32)],
        compiler_params=pltpu.CompilerParams(vmem_limit_bytes=16 * MIB),
        cost_estimate=pl.CostEstimate(
            flops=2 * 8 * units * rows * width,
            bytes_accessed=16 * units * width,
            transcendentals=2 * units * rows,
        ),
        name="gate_up_silu",
    )(direct, start, *weights)


def _down_kernel(h0, h1, h2, h3, d0, d1, own, s1, s2, s3, ht):
    _, _, _, l, c = _place()
    units = h0.shape[0] // 2
    for k, part in enumerate((h0, h1, h2, h3)):
        base = lax.rem(l + k, 4) * (2 * units)
        for i, core in enumerate((c, 1 - c)):
            row = pl.multiple_of(base + core * units, 16)
            ht[pl.ds(row, units), :] = part[pl.ds(i * units, units), :]
    hidden = ht[...].T
    half = hidden.shape[0] // 2
    group = half // 4
    for i, d in enumerate((d0, d1)):
        result = jnp.dot(hidden, d[...], preferred_element_type=F32)
        for k, out in enumerate((own, s1, s2, s3)):
            for j in range(2):
                rows = result[j * half + k * group : j * half + (k + 1) * group]
                out[i, j * group : (j + 1) * group, :] = rows.astype(out.dtype)


def _down(hs, d0, d1):
    rows = hs[0].shape[1]
    depth, width = d0.shape
    block = rows // 4
    send = jax.ShapeDtypeStruct((2, block, width), BF16)
    return pl.pallas_call(
        _down_kernel,
        in_specs=[VMEM] * 6,
        out_specs=[VMEM] * 4,
        out_shape=[jax.ShapeDtypeStruct((2, block, width), F32), send, send, send],
        scratch_shapes=[pltpu.VMEM((depth, rows), BF16)],
        compiler_params=pltpu.CompilerParams(vmem_limit_bytes=24 * MIB),
        cost_estimate=pl.CostEstimate(
            flops=4 * rows * depth * width, bytes_accessed=4 * depth * width, transcendentals=0
        ),
        name="down",
    )(*hs, d0, d1)


def _sum_first_kernel(own, g1, g2, g3, kept, s1, s2, s3):
    x, y, _, _, c = _place()
    _, second = _along(c, x, y)
    for k, out in enumerate((kept, s1, s2, s3)):
        rows = pl.ds(pl.multiple_of(lax.rem(second + k, 4) * 16, 16), 16)
        total = own[:, rows, :]
        for g in (g1, g2, g3):
            total = total + g[:, rows, :].astype(F32)
        out[...] = total.astype(out.dtype)


def _sum_first(own, got):
    width = own.shape[-1]
    send = jax.ShapeDtypeStruct((2, 16, width), BF16)
    return pl.pallas_call(
        _sum_first_kernel,
        in_specs=[VMEM] * 4,
        out_specs=[VMEM] * 4,
        out_shape=[jax.ShapeDtypeStruct((2, 16, width), F32), send, send, send],
        compiler_params=pltpu.CompilerParams(vmem_limit_bytes=8 * MIB),
        name="sum_first",
    )(own, *got)


def _sum_second_kernel(own, g1, g2, g3, here, there):
    _, _, h, _, _ = _place()
    total = own[...]
    for g in (g1, g2, g3):
        total = total + g[...].astype(F32)
    low, high = total[:, :8], total[:, 8:]
    here[...] = jnp.where(h == 0, low, high)
    send = jnp.where(h == 0, high, low)
    there[...] = jnp.concatenate([send[0], send[1]], axis=0).astype(BF16)


def _sum_second(own, got):
    width = own.shape[-1]
    return pl.pallas_call(
        _sum_second_kernel,
        in_specs=[VMEM] * 4,
        out_specs=[VMEM] * 2,
        out_shape=[jax.ShapeDtypeStruct((2, 8, width), F32), jax.ShapeDtypeStruct((16, width), BF16)],
        compiler_params=pltpu.CompilerParams(vmem_limit_bytes=8 * MIB),
        name="sum_second",
    )(own, *got)


def _sum_last_kernel(here, got, own, cross):
    total = got[...].astype(F32)
    own[...] = here[0] + total[:8]
    cross[...] = here[1] + total[8:]


def _sum_last(here, got):
    part = jax.ShapeDtypeStruct((8, got.shape[-1]), F32)
    return pl.pallas_call(
        _sum_last_kernel,
        in_specs=[VMEM] * 2,
        out_specs=[VMEM] * 2,
        out_shape=[part, part],
        compiler_params=pltpu.CompilerParams(vmem_limit_bytes=8 * MIB),
        name="sum_last",
    )(here, got)


def local(tokens, gate_weight, up_weight, down_weight):
    core = lax.axis_index("c")
    swapped = _permute(tokens, _swap)
    quarter, whole = _join(_mine(tokens), swapped)
    near = _permute(quarter, _up_or_down(1))
    two = _permute(quarter, _z_two)
    gate_in, up_in, down_in, _ = lax.optimization_barrier((gate_weight, up_weight, down_weight, quarter))
    gate_other = _permute(gate_in, _swap)
    up_other = _permute(up_in, _swap)
    down_other = _permute(down_in, _swap)
    weights = (gate_weight, gate_other, up_weight, up_other)
    later, near, two = lax.optimization_barrier((whole, near, two))
    direct = _permute(later, _up_or_down(-1))

    packed = _pack((near, two))
    packed, gate_other, up_other, down_other = lax.optimization_barrier(
        (packed, gate_other, up_other, down_other)
    )
    first_back, first_on, second_back, second_on = packed
    around = [
        _permute(first_back, _first(-1)),
        _permute(first_on, _first(1)),
        _permute(second_back, _second(-1)),
        _permute(second_on, _second(1)),
    ]
    whole, _ = lax.optimization_barrier((whole, packed))
    start = _own(whole, weights)

    start = _around((near, two), around, start, weights)
    hidden = _hidden(direct, start, weights)
    two, one, three = (_permute(hidden, _lo(-k)) for k in (2, 1, 3))

    own, *sends = _down((hidden, one, two, three), down_weight, down_other)
    own, *sends = _sum_first(own, [_permute(sends[k - 1], _first(k)) for k in (2, 1, 3)])
    here, there = _sum_second(own, [_permute(sends[k - 1], _second(k)) for k in (2, 1, 3)])
    own, cross = _sum_last(here, _permute(there, _z(4)))
    cross = _permute(cross, _swap)
    mine = lax.broadcasted_iota(jnp.int32, (2, 1, 1), 0) == core
    return jnp.where(mine, own[None], cross[None]).astype(BF16)


def solution(mesh):
    fine = Mesh(mesh.devices.reshape(SIZES), AXES)
    wide, narrow = ("x", "y", "h"), ("l", "c")
    return jax.shard_map(
        local,
        mesh=fine,
        in_specs=(
            P(None, None, narrow),
            P(wide + narrow, None),
            P(wide + narrow, None),
            P(wide, narrow),
        ),
        out_specs=P(None, wide, narrow),
        check_vma=False,
    )
```

```python
import jax
import jax.numpy as jnp
import numpy as np
from jax import lax
from jax.experimental import pallas as pl
from jax.experimental.pallas import tpu as pltpu
from jax.sharding import Mesh, PartitionSpec as P

AXES = ("x", "y", "h", "l", "c")
SIZES = (4, 4, 2, 4, 2)
F32 = jnp.float32
BF16 = jnp.bfloat16
MIB = 1 << 20


def _perm(move):
    pairs = []
    for source in range(256):
        x, y, h, l, c = (int(i) for i in np.unravel_index(source, SIZES))
        X, Y, Z, C = move(x, y, h * 4 + l, c)
        Z %= 8
        pairs.append((source, int(np.ravel_multi_index((X % 4, Y % 4, Z // 4, Z % 4, C % 2), SIZES))))
    return pairs


def _permute(a, move):
    return lax.ppermute(a, AXES, _perm(move))


def _first(k):
    return lambda x, y, z, c: (x + k, y, z, c) if c == 0 else (x, y + k, z, c)


def _second(k):
    return lambda x, y, z, c: (x, y + k, z, c) if c == 0 else (x + k, y, z, c)


def _swap(x, y, z, c):
    return (x, y, z, 1 - c)


def _z(k):
    return lambda x, y, z, c: (x, y, z + k, c)


def _up_or_down(k):
    return lambda x, y, z, c: (x, y, z + k if c == 0 else z - k, c)


def _z_two(x, y, z, c):
    return (x, y, z + 2 if z % 2 == 0 else z - 2, c)


def _lo(k):
    return lambda x, y, z, c: (x, y, (z // 4) * 4 + (z % 4 + k) % 4, c)


def _only(core, move):
    return [(s, d) for s, d in _perm(move) if s % 2 == core]


VMEM = pl.BlockSpec(memory_space=pltpu.VMEM)
NT = (((1,), (1,)), ((), ()))


def _place():
    return [lax.axis_index(a).astype(jnp.int32) for a in AXES]


def _along(core, x, y):
    return jnp.where(core == 0, x, y), jnp.where(core == 0, y, x)


def _order(tokens, out):
    x, y, _, _, c = _place()
    first, second = _along(c, x, y)
    for half, q in enumerate((first + 2 * second, 2 * first + second)):
        for i in range(4):
            a = lax.rem(q + i, 4)
            base = 64 + half * 96 + (i - 1) * 32 if i else half * 32
            for j in range(2):
                b = 2 * half + j
                block = jnp.where(c == 0, a * 4 + b, b * 4 + a)
                row = pl.multiple_of(block * 16, 16)
                out[pl.ds(base + j * 16, 16), :] = tokens[c, pl.ds(row, 16), :]


def _mine_kernel(tokens, mine):
    _order(tokens, mine)


def _mine(tokens):
    _, rows, width = tokens.shape
    return pl.pallas_call(
        _mine_kernel,
        in_specs=[VMEM],
        out_specs=VMEM,
        out_shape=jax.ShapeDtypeStruct((rows, width), BF16),
        compiler_params=pltpu.CompilerParams(vmem_limit_bytes=8 * MIB),
        name="order_own",
    )(tokens)


def _join_kernel(mine, swapped, quarter, whole):
    lead = quarter.shape[1]
    whole[0] = mine[...]
    _order(swapped, whole.at[1])
    quarter[0] = mine[:lead]
    quarter[1] = whole[1, :lead]


def _join(mine, swapped):
    rows, width = mine.shape
    return pl.pallas_call(
        _join_kernel,
        in_specs=[VMEM] * 2,
        out_specs=[VMEM] * 2,
        out_shape=[
            jax.ShapeDtypeStruct((2, rows // 4, width), BF16),
            jax.ShapeDtypeStruct((2, rows, width), BF16),
        ],
        compiler_params=pltpu.CompilerParams(vmem_limit_bytes=8 * MIB),
        name="order_other",
    )(mine, swapped)


def _weight_columns(weights, block, width):
    column = pl.multiple_of(block * width, 128)
    return jnp.concatenate([w[:, pl.ds(column, width)] for w in weights], axis=0)


def _in_order(rows):
    return jnp.concatenate([rows[:32], rows[64:160], rows[32:64], rows[160:]], axis=0)


def _own_kernel(whole, g0, g1, u0, u1, out):
    _, _, _, l, c = _place()
    width = whole.shape[-1]
    for k in range(2):
        w = _weight_columns((g0, g1, u0, u1), 2 * l + (c if k == 0 else 1 - c), width)
        part = lax.dot_general(w, _in_order(whole[k]), NT, preferred_element_type=F32)
        if k == 0:
            out[...] = part
        else:
            out[...] += part


def _own(whole, weights):
    units, (_, rows, width) = weights[0].shape[0], whole.shape
    return pl.pallas_call(
        _own_kernel,
        in_specs=[VMEM] * 5,
        out_specs=VMEM,
        out_shape=jax.ShapeDtypeStruct((4 * units, rows), F32),
        compiler_params=pltpu.CompilerParams(vmem_limit_bytes=16 * MIB),
        cost_estimate=pl.CostEstimate(
            flops=2 * 8 * units * rows * width, bytes_accessed=20 * units * width, transcendentals=0
        ),
        name="own_features",
    )(whole, *weights)


def _pack_kernel(near, two, first_back, first_on, second_back, second_on):
    for i, piece in enumerate((near, two)):
        for j in range(2):
            k = 2 * i + j
            a, b = piece[j, :32], piece[j, 32:]
            first_back[k] = jnp.concatenate([a, b[:16]], axis=0)
            first_on[k] = jnp.concatenate([a, b[16:]], axis=0)
            second_back[k] = jnp.concatenate([a[:16], b], axis=0)
            second_on[k] = jnp.concatenate([a[16:], b], axis=0)


def _pack(pieces):
    send = jax.ShapeDtypeStruct((4, 48, pieces[0].shape[-1]), BF16)
    return pl.pallas_call(
        _pack_kernel,
        in_specs=[VMEM] * 2,
        out_specs=[VMEM] * 4,
        out_shape=[send] * 4,
        compiler_params=pltpu.CompilerParams(vmem_limit_bytes=16 * MIB),
        name="pack_quarters",
    )(*pieces)


def _around_kernel(near, two, p1, m1, p2, m2, start, g0, g1, u0, u1, out):
    _, _, _, l, c = _place()
    width = near.shape[-1]
    ahead = (jnp.where(c == 0, 3, 1), 2)
    for k in range(4):
        block = 2 * lax.rem(l + ahead[k // 2], 4) + (c if k % 2 == 0 else 1 - c)
        w = _weight_columns((g0, g1, u0, u1), block, width)
        kept = (near, two)[k // 2][k % 2]
        t = jnp.concatenate(
            [
                kept[:32],
                p1[k, :32],
                p2[k, :16],
                m2[k, :16],
                m1[k, :32],
                kept[32:],
                p2[k, 16:],
                p1[k, 32:],
                m1[k, 32:],
                m2[k, 16:],
            ],
            axis=0,
        )
        part = lax.dot_general(w, t, NT, preferred_element_type=F32)
        if k == 0:
            out[...] = start[...] + part
        else:
            out[...] += part


def _around(kept, around, start, weights):
    units, width = weights[0].shape[0], kept[0].shape[-1]
    rows = start.shape[1]
    return pl.pallas_call(
        _around_kernel,
        in_specs=[VMEM] * 11,
        out_specs=VMEM,
        out_shape=jax.ShapeDtypeStruct(start.shape, F32),
        compiler_params=pltpu.CompilerParams(vmem_limit_bytes=16 * MIB),
        cost_estimate=pl.CostEstimate(
            flops=2 * 16 * units * rows * width, bytes_accessed=32 * units * width, transcendentals=0
        ),
        name="gate_up_around",
    )(*kept, *around, start, *weights)


def _hidden_kernel(direct, start, g0, g1, u0, u1, out, acc):
    x, y, _, l, c = _place()
    first, second = _along(c, x, y)
    width = direct.shape[-1]
    units = g0.shape[0]
    for k in range(2):
        block = 2 * lax.rem(l + jnp.where(c == 0, 1, 3), 4) + (c if k == 0 else 1 - c)
        w = _weight_columns((g0, g1, u0, u1), block, width)
        part = lax.dot_general(w, _in_order(direct[k]), NT, preferred_element_type=F32)
        if k == 0:
            acc[...] = start[...] + part
        else:
            acc[...] += part
    gate = acc[pl.ds(0, 2 * units), :]
    up = acc[pl.ds(2 * units, 2 * units), :]
    hidden = gate / (1 + jnp.exp(-gate)) * up
    half = hidden.shape[1] // 2
    group = half // 4
    turns = (2 * lax.rem(second, 2), lax.rem(first + second, 4))
    for i, turn in enumerate(turns):
        part = pltpu.roll(hidden[:, i * half : (i + 1) * half], turn * group, 1)
        out[:, i * half : (i + 1) * half] = part.astype(BF16)


def _hidden(direct, start, weights):
    units, (_, rows, width) = weights[0].shape[0], direct.shape
    return pl.pallas_call(
        _hidden_kernel,
        in_specs=[VMEM] * 6,
        out_specs=VMEM,
        out_shape=jax.ShapeDtypeStruct((2 * units, rows), BF16),
        scratch_shapes=[pltpu.VMEM((4 * units, rows), F32)],
        compiler_params=pltpu.CompilerParams(vmem_limit_bytes=16 * MIB),
        cost_estimate=pl.CostEstimate(
            flops=2 * 8 * units * rows * width,
            bytes_accessed=16 * units * width,
            transcendentals=2 * units * rows,
        ),
        name="gate_up_silu",
    )(direct, start, *weights)


def _down_part(hidden, ahead, d, ht):
    _, _, _, l, c = _place()
    units = hidden[0].shape[0] // 2
    for n, part in enumerate(hidden):
        for i, core in enumerate((c, 1 - c)):
            row = pl.multiple_of(n * 2 * units + core * units, 16)
            ht[pl.ds(row, units), :] = part[pl.ds(i * units, units), :]
    left = ht[...].T
    starts = [pl.multiple_of(lax.rem(l + k, 4) * 2 * units, 16) for k in ahead]
    for i, w in enumerate(d):
        right = jnp.concatenate([w[pl.ds(row, 2 * units), :] for row in starts], axis=0)
        yield i, jnp.dot(left, right, preferred_element_type=F32)


def _down_near_kernel(h0, h1, d0, d1, out, ht):
    for i, result in _down_part((h0, h1), (0, 1), (d0, d1), ht):
        out[i] = result


def _down_far_kernel(h2, h3, near, d0, d1, own, s1, s2, s3, ht):
    for i, result in _down_part((h2, h3), (2, 3), (d0, d1), ht):
        result = near[i] + result
        half = result.shape[0] // 2
        group = half // 4
        for k, out in enumerate((own, s1, s2, s3)):
            for j in range(2):
                rows = result[j * half + k * group : j * half + (k + 1) * group]
                out[i, j * group : (j + 1) * group, :] = rows.astype(out.dtype)


def _down(hs, d0, d1):
    units, rows = hs[0].shape
    depth, width = d0.shape
    block = rows // 4
    send = jax.ShapeDtypeStruct((2, block, width), BF16)
    common = dict(
        scratch_shapes=[pltpu.VMEM((2 * units, rows), BF16)],
        compiler_params=pltpu.CompilerParams(vmem_limit_bytes=16 * MIB),
        cost_estimate=pl.CostEstimate(
            flops=2 * rows * depth * width, bytes_accessed=2 * depth * width, transcendentals=0
        ),
    )
    near = pl.pallas_call(
        _down_near_kernel,
        in_specs=[VMEM] * 4,
        out_specs=VMEM,
        out_shape=jax.ShapeDtypeStruct((2, rows, width), F32),
        name="down_near",
        **common,
    )(hs[0], hs[1], d0, d1)
    return pl.pallas_call(
        _down_far_kernel,
        in_specs=[VMEM] * 5,
        out_specs=[VMEM] * 4,
        out_shape=[jax.ShapeDtypeStruct((2, block, width), F32), send, send, send],
        name="down_far",
        **common,
    )(hs[2], hs[3], near, d0, d1)


def _sum_first_kernel(own, g1, g2, g3, kept, s1, s2, s3):
    x, y, _, _, c = _place()
    _, second = _along(c, x, y)
    for k, out in enumerate((kept, s1, s2, s3)):
        rows = pl.ds(pl.multiple_of(lax.rem(second + k, 4) * 16, 16), 16)
        total = own[:, rows, :]
        for g in (g1, g2, g3):
            total = total + g[:, rows, :].astype(F32)
        out[...] = total.astype(out.dtype)


def _sum_first(own, got):
    width = own.shape[-1]
    send = jax.ShapeDtypeStruct((2, 16, width), BF16)
    return pl.pallas_call(
        _sum_first_kernel,
        in_specs=[VMEM] * 4,
        out_specs=[VMEM] * 4,
        out_shape=[jax.ShapeDtypeStruct((2, 16, width), F32), send, send, send],
        compiler_params=pltpu.CompilerParams(vmem_limit_bytes=8 * MIB),
        name="sum_first",
    )(own, *got)


def _sum_second_kernel(own, g1, g2, g3, here, there):
    _, _, h, _, _ = _place()
    total = own[...]
    for g in (g1, g2, g3):
        total = total + g[...].astype(F32)
    low, high = total[:, :8], total[:, 8:]
    here[...] = jnp.where(h == 0, low, high)
    send = jnp.where(h == 0, high, low)
    there[...] = jnp.concatenate([send[0], send[1]], axis=0).astype(BF16)


def _sum_second(own, got):
    width = own.shape[-1]
    return pl.pallas_call(
        _sum_second_kernel,
        in_specs=[VMEM] * 4,
        out_specs=[VMEM] * 2,
        out_shape=[jax.ShapeDtypeStruct((2, 8, width), F32), jax.ShapeDtypeStruct((16, width), BF16)],
        compiler_params=pltpu.CompilerParams(vmem_limit_bytes=8 * MIB),
        name="sum_second",
    )(own, *got)


def _sum_last_kernel(here, got, own, cross):
    total = got[...].astype(F32)
    own[...] = here[0] + total[:8]
    cross[...] = here[1] + total[8:]


def _sum_last(here, got):
    part = jax.ShapeDtypeStruct((8, got.shape[-1]), F32)
    return pl.pallas_call(
        _sum_last_kernel,
        in_specs=[VMEM] * 2,
        out_specs=[VMEM] * 2,
        out_shape=[part, part],
        compiler_params=pltpu.CompilerParams(vmem_limit_bytes=8 * MIB),
        name="sum_last",
    )(here, got)


def local(tokens, gate_weight, up_weight, down_weight):
    core = lax.axis_index("c")
    swapped = _permute(tokens, _swap)
    quarter, whole = _join(_mine(tokens), swapped)
    near = _permute(quarter, _up_or_down(1))
    two = _permute(quarter, _z_two)
    gate_in, up_in, down_in, _ = lax.optimization_barrier((gate_weight, up_weight, down_weight, quarter))
    gate_other = _permute(gate_in, _swap)
    up_other = _permute(up_in, _swap)
    down_other = _permute(down_in, _swap)
    weights = (gate_weight, gate_other, up_weight, up_other)
    later, near, two = lax.optimization_barrier((whole, near, two))
    direct = _permute(later, _up_or_down(-1))

    packed = _pack((near, two))
    packed, gate_other, up_other, down_other = lax.optimization_barrier(
        (packed, gate_other, up_other, down_other)
    )
    first_back, first_on, second_back, second_on = packed
    around = [
        _permute(first_back, _first(-1)),
        _permute(first_on, _first(1)),
        _permute(second_back, _second(-1)),
        _permute(second_on, _second(1)),
    ]
    whole, _ = lax.optimization_barrier((whole, packed))
    start = _own(whole, weights)

    start = _around((near, two), around, start, weights)
    hidden = _hidden(direct, start, weights)
    two, one, three = (_permute(hidden, _lo(-k)) for k in (2, 1, 3))

    own, *sends = _down((hidden, one, two, three), down_weight, down_other)
    own, *sends = _sum_first(own, [_permute(sends[k - 1], _first(k)) for k in (2, 1, 3)])
    here, there = _sum_second(own, [_permute(sends[k - 1], _second(k)) for k in (2, 1, 3)])
    own, cross = _sum_last(here, _permute(there, _z(4)))
    cross = _permute(cross, _swap)
    mine = lax.broadcasted_iota(jnp.int32, (2, 1, 1), 0) == core
    return jnp.where(mine, own[None], cross[None]).astype(BF16)


def solution(mesh):
    fine = Mesh(mesh.devices.reshape(SIZES), AXES)
    wide, narrow = ("x", "y", "h"), ("l", "c")
    return jax.shard_map(
        local,
        mesh=fine,
        in_specs=(
            P(None, None, narrow),
            P(wide + narrow, None),
            P(wide + narrow, None),
            P(wide, narrow),
        ),
        out_specs=P(None, wide, narrow),
        check_vma=False,
    )
```
